32 devices in a mesh: dom: 8 (over z, x), wide: 4 (over y, core).
Axes of the slice: x: 2, y: 2, z: 4, core: 2. Of those that a mesh axis runs over, the one named last changes fastest.
Arguments:
- features: bfloat16 [8192, 512], P(('dom', 'wide')), may hold values from -6 to 6
- w_self: bfloat16 [512, 512], replicated, may hold values from -0.25 to 0.25
- w_neigh: bfloat16 [512, 512], replicated, may hold values from -0.25 to 0.25
- boundary: int32 [32, 2, 64], P(('dom', 'wide')), may hold values from 0 to 255
- neighbors: int32 [8192, 16], P(('dom', 'wide')), may hold values from 0 to 384, as said below
- anchors: int32 [128, 32], P(('dom', 'wide')), may hold values from 0 to 255
- negatives: int32 [128, 32, 8], P(('dom', 'wide')), may hold values from 0 to 255
- positives: int32 [8192, 2], P(('dom', 'wide')), may hold values from 0 to 255
Outputs:
- embed: bfloat16 [8192, 512], P(('dom', 'wide'))
- embed_grad: bfloat16 [8192, 512], P(('dom', 'wide'))
The draws below stay inside these ranges and needn't reach their ends.
Inputs may be any that keep to these rules, and one draw needn't show every extreme that they name: `neighbors`: each row has its live slots first, 1 to 16 of them; the first node of every partition has 16; slots after the live ones hold 384. `anchors`: rows of the own partition. `negatives`: rows of the own partition. `positives`: rows of the own partition.
All inputs are finite; a program needn't handle non-finite values.
Results may differ from the reference program's by a relative error of at most 0.0053.
Values may be sent and summed in bfloat16 or wider, within the bound.
A program may use at most 64 MiB of HBM per device.

```python
import math
import jax
import jax.numpy as jnp
from jax import lax

D = 512
NODE_DEV = 256
DEG = 16
ANCH = 32
K = 8
BND = 64
TABLE = 384
NODES = 8192
N_DOM = 8
N_WIDE = 4


def draw_neighbors(key, part):
    key_deg, key_idx = jax.random.split(jax.random.fold_in(key, 11))
    degree = jax.random.randint(key_deg, (NODES, 1), 1, DEG + 1)
    rows = jnp.arange(NODES)[:, None]
    degree = jnp.where(rows % NODE_DEV == 0, DEG, degree)
    index = jax.random.randint(key_idx, (NODES, DEG), 0, TABLE)
    slots = jnp.arange(DEG)[None, :]
    return jnp.where(slots < degree, index, TABLE).astype(jnp.int32)


def place_ends(values, key, low, largest):
    index_at = [jax.random.randint(jax.random.fold_in(key, axis), (), 0, length) for axis, length in enumerate(values.shape)]
    longest = values.shape.index(max(values.shape))
    neighbour = index_at[:longest] + [(index_at[longest] + 1) % values.shape[longest]] + index_at[longest + 1:]
    return values.at[tuple(index_at)].set(low).at[tuple(neighbour)].set(largest)


def block_levels(key, shape, cuts, least, high):
    gain = 1.0
    for position, shards_of in cuts:
        steps = jax.random.uniform(jax.random.fold_in(jax.random.fold_in(key, 6), position), (shards_of,), jnp.float32, least / len(cuts), high / len(cuts))
        gain = gain * jnp.repeat(jnp.exp(steps), shape[position] // shards_of).reshape((-1,) + (1,) * (len(shape) - 1 - position))
    return gain


def normal_values(stream_key, extent, deviation, bound, pieces=(), kind=jnp.bfloat16):
    result = deviation * jax.random.normal(stream_key, extent, jnp.float32)
    if pieces:
        result = result * block_levels(stream_key, extent, pieces, -0.22, 0.18)
    return jnp.clip(result, -bound, bound).astype(kind)


def setup_inputs(seed: int = 0) -> dict:
    key_of = jax.random.split(jax.random.key(seed), 9)
    features = normal_values(key_of[0], (NODES, D), 1.0, 6.0, ((0, 32),))
    w_self = normal_values(key_of[1], (D, D), D ** -0.5, 0.25)
    w_neigh = normal_values(key_of[2], (D, D), D ** -0.5, 0.25)
    boundary = place_ends(jax.random.randint(key_of[3], (N_DOM * N_WIDE, 2, BND), 0, NODE_DEV), jax.random.fold_in(key_of[3], 1), 0, NODE_DEV - 1).astype(jnp.int32)
    neighbors = draw_neighbors(jax.random.fold_in(key_of[8], 71), 0)
    anchors = place_ends(jax.random.randint(key_of[5], (N_DOM * N_WIDE * N_WIDE, ANCH), 0, NODE_DEV), jax.random.fold_in(key_of[5], 1), 0, NODE_DEV - 1).astype(jnp.int32)
    negatives = place_ends(jax.random.randint(key_of[6], (N_DOM * N_WIDE * N_WIDE, ANCH, K), 0, NODE_DEV), jax.random.fold_in(key_of[6], 1), 0, NODE_DEV - 1).astype(jnp.int32)
    positives = place_ends(jax.random.randint(key_of[7], (NODES, 2), 0, NODE_DEV), jax.random.fold_in(key_of[7], 1), 0, NODE_DEV - 1).astype(jnp.int32)
    return {"features": features, "w_self": w_self, "w_neigh": w_neigh, "boundary": boundary, "neighbors": neighbors, "anchors": anchors, "negatives": negatives, "positives": positives}


def reference(features, w_self, w_neigh, boundary, neighbors, anchors, negatives, positives):
    scale = 1.0 / math.sqrt(D)
    parts = N_DOM * N_WIDE
    xs = features.reshape(N_DOM, N_WIDE, NODE_DEV, D)
    bnd = boundary.reshape(N_DOM, N_WIDE, 2, BND)
    take = jax.vmap(jax.vmap(lambda x, i: x[i]))
    upward = take(xs, bnd[:, :, 0])
    downward = take(xs, bnd[:, :, 1])
    zero_rows = jnp.zeros_like(upward[:1])
    below = jnp.concatenate([zero_rows, upward[:-1]], axis=0)
    above = jnp.concatenate([downward[1:], zero_rows], axis=0)
    pad_row = jnp.zeros((N_DOM, N_WIDE, 1, D), jnp.bfloat16)
    tables = jnp.concatenate([xs, below, above, pad_row], axis=2).reshape(parts, TABLE + 1, D)
    nbrs = neighbors.reshape(parts, NODE_DEV, DEG)
    feats = features.reshape(parts, NODE_DEV, D)

    def layer(args):
        table, nbr, own = args
        summed = lax.optimization_barrier(jnp.sum(table[nbr].astype(jnp.float32), axis=1))
        degree = lax.optimization_barrier(jnp.sum((nbr < TABLE).astype(jnp.float32), axis=1))
        mean = (summed / degree[:, None]).astype(jnp.bfloat16)
        out = jnp.dot(own, w_self, preferred_element_type=jnp.float32) + jnp.dot(mean, w_neigh, preferred_element_type=jnp.float32)
        return out.astype(jnp.bfloat16)
    embed = lax.map(layer, (tables, nbrs, feats))
    hs = embed.reshape(N_DOM, N_WIDE, NODE_DEV, D)
    anc = anchors.reshape(N_DOM, N_WIDE, N_WIDE, ANCH)
    neg = negatives.reshape(N_DOM, N_WIDE, N_WIDE, ANCH, K)
    pos = positives.reshape(N_DOM, N_WIDE, NODE_DEV, 2)
    pick = jax.vmap(lambda g, i: g[i])

    def per_part(t):
        dom_i = t // N_WIDE
        wide_i = t % N_WIDE
        group = hs[dom_i]
        mine = group[wide_i]
        group_anc = anc[dom_i]
        group_neg = neg[dom_i]
        a_rows = mine[group_anc[wide_i]].astype(jnp.float32)
        r_rows = pick(group, group_neg[:, wide_i]).astype(jnp.float32)
        coef = jax.nn.sigmoid(jnp.einsum('jad,jakd->jak', a_rows, r_rows) * scale)
        anchor_terms = jnp.einsum('jak,jakd->jad', coef, r_rows)
        grad = jax.ops.segment_sum(anchor_terms.reshape(-1, D), group_anc[wide_i].reshape(-1), NODE_DEV)
        s_rows = pick(group, group_anc[:, wide_i]).astype(jnp.float32)
        o_rows = mine[group_neg[wide_i]].astype(jnp.float32)
        coef2 = jax.nn.sigmoid(jnp.einsum('vad,vakd->vak', s_rows, o_rows) * scale)
        owner_terms = coef2[..., None] * s_rows[:, :, None, :]
        grad = grad + jax.ops.segment_sum(owner_terms.reshape(-1, D), group_neg[wide_i].reshape(-1), NODE_DEV)
        pairs = pos[dom_i, wide_i]
        hu = mine[pairs[:, 0]].astype(jnp.float32)
        hv = mine[pairs[:, 1]].astype(jnp.float32)
        coef3 = jax.nn.sigmoid(lax.optimization_barrier(jnp.sum(hu * hv, axis=1)) * scale) - 1.0
        grad = grad + jax.ops.segment_sum(coef3[:, None] * hv, pairs[:, 0], NODE_DEV)
        grad = grad + jax.ops.segment_sum(coef3[:, None] * hu, pairs[:, 1], NODE_DEV)
        return grad.astype(jnp.bfloat16)
    grads = lax.map(per_part, jnp.arange(parts, dtype=jnp.int32))
    return (embed.reshape(NODES, D), grads.reshape(NODES, D))
```

```python
import functools
import math

import jax
import jax.numpy as jnp
from jax import lax
from jax.experimental import pallas as pl
from jax.experimental.pallas import tpu as pltpu
from jax.sharding import PartitionSpec as P

MESH = pl.DeviceIdType.MESH
BF = jnp.bfloat16
F32 = jnp.float32


def dot(a, b):
    return jnp.dot(a, b, preferred_element_type=F32)


def dot_nt(a, b):
    return lax.dot_general(a, b, (((1,), (1,)), ((), ())), preferred_element_type=F32)


def dot_tn(a, b):
    return lax.dot_general(a, b, (((0,), (0,)), ((), ())), preferred_element_type=F32)


def marks(row, height):
    rows = lax.broadcasted_iota(jnp.int32, (height, row.shape[1]), 0)
    return jnp.where(rows == row, 1.0, 0.0)


def kernel(
    n_dom,
    n_wide,
    feat_in,
    ws_in,
    wn_in,
    bnd_in,
    nbr_in,
    anch_in,
    neg_in,
    pos_in,
    embed_out,
    grad_out,
    feat,
    ws,
    wn,
    bnd,
    nbr,
    anch,
    neg,
    pos,
    b_send,
    b_recv,
    a_send,
    a_recv,
    t_send,
    t_recv,
    embed_v,
    grad_v,
    own_sum,
    own_proj,
    load_sem,
    store_sem,
    bs_sem,
    br_sem,
    as_sem,
    ar_sem,
    ts_sem,
    tr_sem,
):
    node_dev, width = feat.shape
    slots = nbr.shape[0]
    bnd_rows = bnd.shape[2]
    peers, anch_n = anch.shape
    fan = neg.shape[1]
    scale = 1.0 / math.sqrt(width)
    d = lax.axis_index("dom")
    w = lax.axis_index("wide")
    has_prev = d > 0
    has_next = d < n_dom - 1

    loads = [
        pltpu.make_async_copy(src, dst, load_sem.at[i])
        for i, (src, dst) in enumerate(
            [
                (bnd_in, bnd),
                (feat_in, feat),
                (nbr_in, nbr),
                (anch_in, anch),
                (neg_in, neg),
                (pos_in, pos),
                (ws_in, ws),
                (wn_in, wn),
            ]
        )
    ]
    for load in loads:
        load.start()

    barrier = pltpu.get_barrier_semaphore()

    @pl.when(has_prev)
    def _():
        pl.semaphore_signal(barrier, inc=1, device_id=(d - 1, w), device_id_type=MESH)

    @pl.when(has_next)
    def _():
        pl.semaphore_signal(barrier, inc=1, device_id=(d + 1, w), device_id_type=MESH)

    partner = [lax.rem(w + o, n_wide) for o in range(n_wide)]
    for o in range(1, n_wide):
        pl.semaphore_signal(barrier, inc=1, device_id=(d, partner[o]), device_id_type=MESH)

    loads[0].wait()
    loads[1].wait()
    features = feat[...]
    b_send[0] = dot_tn(marks(bnd[0, 0:1, :], node_dev).astype(BF), features).astype(BF)
    b_send[1] = dot_tn(marks(bnd[0, 1:2, :], node_dev).astype(BF), features).astype(BF)

    arrivals = n_wide - 1 + has_prev.astype(jnp.int32) + has_next.astype(jnp.int32)
    pl.semaphore_wait(barrier, arrivals)

    up = pltpu.make_async_remote_copy(
        src_ref=b_send.at[0],
        dst_ref=b_recv.at[0],
        send_sem=bs_sem.at[0],
        recv_sem=br_sem.at[0],
        device_id=(d + 1, w),
        device_id_type=MESH,
    )
    down = pltpu.make_async_remote_copy(
        src_ref=b_send.at[1],
        dst_ref=b_recv.at[1],
        send_sem=bs_sem.at[1],
        recv_sem=br_sem.at[1],
        device_id=(d - 1, w),
        device_id_type=MESH,
    )

    @pl.when(has_next)
    def _():
        up.start()

    @pl.when(has_prev)
    def _():
        down.start()

    @pl.when(jnp.logical_not(has_prev))
    def _():
        b_recv[0] = jnp.zeros((bnd_rows, width), BF)

    @pl.when(jnp.logical_not(has_next))
    def _():
        b_recv[1] = jnp.zeros((bnd_rows, width), BF)

    loads[2].wait()
    table_rows = node_dev + 2 * bnd_rows
    counts_t = marks(nbr[0:1, :], table_rows)
    for slot in range(1, slots):
        counts_t = counts_t + marks(nbr[slot : slot + 1, :], table_rows)
    counts = counts_t.T
    inverse = 1.0 / jnp.sum(counts, axis=1, keepdims=True)
    counts = counts.astype(BF)
    own_sum[...] = dot(counts[:, :node_dev], features)
    counts_bnd = counts[:, node_dev:]

    loads[6].wait()
    own_proj[...] = dot(features, ws[...])

    loads[3].wait()
    a_row = jnp.concatenate([anch[v : v + 1, :] for v in range(peers)], axis=1)
    anchors_t = marks(a_row, node_dev)
    anchors_n = anchors_t.T.astype(BF)
    anchors_t = anchors_t.astype(BF)

    loads[4].wait()
    n_rows = jnp.concatenate([neg[v] for v in range(peers)], axis=1)
    mult_t = marks(n_rows[0:1, :], node_dev)
    for k in range(1, fan):
        mult_t = mult_t + marks(n_rows[k : k + 1, :], node_dev)
    mult = mult_t.T

    loads[5].wait()
    first = marks(pos[0:1, :], node_dev).astype(BF)
    second = marks(pos[1:2, :], node_dev).astype(BF)
    pairs = dot_nt(
        jnp.concatenate([first, second], axis=1), jnp.concatenate([second, first], axis=1)
    )
    loads[7].wait()

    @pl.when(has_prev)
    def _():
        up.wait_recv()

    @pl.when(has_next)
    def _():
        down.wait_recv()

    received = b_recv[...].reshape(2 * bnd_rows, width)
    mean = ((own_sum[...] + dot(counts_bnd, received)) * inverse).astype(BF)
    embed = (own_proj[...] + dot(mean, wn[...])).astype(BF)
    embed_v[...] = embed

    a_send[...] = dot(anchors_n, embed).astype(BF).reshape(peers, anch_n, width)

    def exchange(source, target, send, recv):
        return [
            pltpu.make_async_remote_copy(
                src_ref=source.at[partner[o]],
                dst_ref=target.at[w],
                send_sem=send.at[o - 1],
                recv_sem=recv.at[o - 1],
                device_id=(d, partner[o]),
                device_id_type=MESH,
            )
            for o in range(1, n_wide)
        ]

    out = exchange(a_send, a_recv, as_sem, ar_sem)
    for copy in out:
        copy.start()
    store_embed = pltpu.make_async_copy(embed_v, embed_out, store_sem.at[0])
    store_embed.start()
    a_recv[pl.ds(w, 1)] = a_send[pl.ds(w, 1)]

    c_pos = pairs * (jax.nn.sigmoid(dot_nt(embed, embed) * scale) - 1.0)
    own_sum[...] = dot(c_pos.astype(BF), embed)

    for copy in out:
        copy.wait_recv()
    got = a_recv[...].reshape(peers * anch_n, width)
    coef = (mult * jax.nn.sigmoid(dot_nt(got, embed) * scale)).astype(BF)
    t_send[...] = dot(coef, embed).astype(BF).reshape(peers, anch_n, width)
    back = exchange(t_send, t_recv, ts_sem, tr_sem)
    for copy in back:
        copy.start()
    t_recv[pl.ds(w, 1)] = t_send[pl.ds(w, 1)]
    own_sum[...] += dot_tn(coef, got)
    for copy in back:
        copy.wait_recv()
    terms = t_recv[...].reshape(peers * anch_n, width)
    grad_v[...] = (own_sum[...] + dot(anchors_t, terms)).astype(BF)
    store_grad = pltpu.make_async_copy(grad_v, grad_out, store_sem.at[1])
    store_grad.start()

    @pl.when(has_next)
    def _():
        up.wait_send()

    @pl.when(has_prev)
    def _():
        down.wait_send()

    for copy in out + back:
        copy.wait_send()
    store_embed.wait()
    store_grad.wait()


def body(n_dom, n_wide, features, w_self, w_neigh, boundary, neighbors, anchors, negatives, positives):
    node_dev, width = features.shape
    bnd_rows = boundary.shape[2]
    peers, anch_n = anchors.shape
    small = [boundary, neighbors.T, anchors, negatives.transpose(0, 2, 1), positives.T]
    block = (peers, anch_n, width)
    anywhere = pl.BlockSpec(memory_space=pl.ANY)
    return pl.pallas_call(
        functools.partial(kernel, n_dom, n_wide),
        out_shape=[jax.ShapeDtypeStruct((node_dev, width), BF)] * 2,
        in_specs=[anywhere] * 8,
        out_specs=[anywhere] * 2,
        scratch_shapes=[
            pltpu.VMEM(features.shape, BF),
            pltpu.VMEM(w_self.shape, BF),
            pltpu.VMEM(w_neigh.shape, BF),
        ]
        + [pltpu.VMEM(x.shape, jnp.int32) for x in small]
        + [pltpu.VMEM((2, bnd_rows, width), BF)] * 2
        + [pltpu.VMEM(block, BF)] * 4
        + [pltpu.VMEM((node_dev, width), BF)] * 2
        + [pltpu.VMEM((node_dev, width), F32)] * 2
        + [
            pltpu.SemaphoreType.DMA((8,)),
            pltpu.SemaphoreType.DMA((2,)),
            pltpu.SemaphoreType.DMA((2,)),
            pltpu.SemaphoreType.DMA((2,)),
        ]
        + [pltpu.SemaphoreType.DMA((n_wide - 1,))] * 4,
        compiler_params=pltpu.CompilerParams(
            collective_id=0, has_side_effects=True, vmem_limit_bytes=32 * 1024 * 1024
        ),
    )(features, w_self, w_neigh, *small)


def solution(mesh):
    return jax.shard_map(
        functools.partial(body, mesh.shape["dom"], mesh.shape["wide"]),
        mesh=mesh,
        in_specs=(
            P(("dom", "wide"), None),
            P(),
            P(),
            P(("dom", "wide"), None, None),
            P(("dom", "wide"), None),
            P(("dom", "wide"), None),
            P(("dom", "wide"), None, None),
            P(("dom", "wide"), None),
        ),
        out_specs=(P(("dom", "wide"), None), P(("dom", "wide"), None)),
        check_vma=False,
    )
```

```python
import functools
import math

import jax
import jax.numpy as jnp
from jax import lax
from jax.experimental import pallas as pl
from jax.experimental.pallas import tpu as pltpu
from jax.sharding import PartitionSpec as P

MESH = pl.DeviceIdType.MESH
BF = jnp.bfloat16
F32 = jnp.float32


def dot(a, b):
    return jnp.dot(a, b, preferred_element_type=F32)


def dot_nt(a, b):
    return lax.dot_general(a, b, (((1,), (1,)), ((), ())), preferred_element_type=F32)


def dot_tn(a, b):
    return lax.dot_general(a, b, (((0,), (0,)), ((), ())), preferred_element_type=F32)


def marks(row, height):
    rows = lax.broadcasted_iota(jnp.int32, (height, row.shape[1]), 0)
    return jnp.where(rows == row, 1.0, 0.0)


def kernel(
    n_dom,
    n_wide,
    feat_in,
    ws_in,
    wn_in,
    bnd_in,
    nbr_in,
    anch_in,
    neg_in,
    pos_in,
    embed_v,
    grad_v,
    feat,
    ws,
    wn,
    bnd,
    nbr,
    anch,
    neg,
    pos,
    b_send,
    b_recv,
    a_send,
    a_recv,
    t_send,
    t_recv,
    own_sum,
    own_proj,
    load_sem,
    bs_sem,
    br_sem,
    as_sem,
    ar_sem,
    ts_sem,
    tr_sem,
):
    node_dev, width = feat.shape
    slots = nbr.shape[0]
    bnd_rows = bnd.shape[2]
    peers, anch_n = anch.shape
    fan = neg.shape[1]
    scale = 1.0 / math.sqrt(width)
    d = lax.axis_index("dom")
    w = lax.axis_index("wide")
    has_prev = d > 0
    has_next = d < n_dom - 1

    loads = [
        pltpu.make_async_copy(src, dst, load_sem.at[i])
        for i, (src, dst) in enumerate(
            [
                (bnd_in, bnd),
                (feat_in, feat),
                (nbr_in, nbr),
                (anch_in, anch),
                (neg_in, neg),
                (pos_in, pos),
                (ws_in, ws),
                (wn_in, wn),
            ]
        )
    ]
    for load in loads:
        load.start()

    barrier = pltpu.get_barrier_semaphore()

    @pl.when(has_prev)
    def _():
        pl.semaphore_signal(barrier, inc=1, device_id=(d - 1, w), device_id_type=MESH)

    @pl.when(has_next)
    def _():
        pl.semaphore_signal(barrier, inc=1, device_id=(d + 1, w), device_id_type=MESH)

    partner = [lax.rem(w + o, n_wide) for o in range(n_wide)]
    for o in range(1, n_wide):
        pl.semaphore_signal(barrier, inc=1, device_id=(d, partner[o]), device_id_type=MESH)

    loads[0].wait()
    loads[1].wait()
    features = feat[...]
    b_send[0] = dot_tn(marks(bnd[0, 0:1, :], node_dev).astype(BF), features).astype(BF)
    b_send[1] = dot_tn(marks(bnd[0, 1:2, :], node_dev).astype(BF), features).astype(BF)

    arrivals = n_wide - 1 + has_prev.astype(jnp.int32) + has_next.astype(jnp.int32)
    pl.semaphore_wait(barrier, arrivals)

    up = pltpu.make_async_remote_copy(
        src_ref=b_send.at[0],
        dst_ref=b_recv.at[0],
        send_sem=bs_sem.at[0],
        recv_sem=br_sem.at[0],
        device_id=(d + 1, w),
        device_id_type=MESH,
    )
    down = pltpu.make_async_remote_copy(
        src_ref=b_send.at[1],
        dst_ref=b_recv.at[1],
        send_sem=bs_sem.at[1],
        recv_sem=br_sem.at[1],
        device_id=(d - 1, w),
        device_id_type=MESH,
    )

    @pl.when(has_next)
    def _():
        up.start()

    @pl.when(has_prev)
    def _():
        down.start()

    @pl.when(jnp.logical_not(has_prev))
    def _():
        b_recv[0] = jnp.zeros((bnd_rows, width), BF)

    @pl.when(jnp.logical_not(has_next))
    def _():
        b_recv[1] = jnp.zeros((bnd_rows, width), BF)

    loads[2].wait()
    table_rows = node_dev + 2 * bnd_rows
    counts_t = marks(nbr[0:1, :], table_rows)
    for slot in range(1, slots):
        counts_t = counts_t + marks(nbr[slot : slot + 1, :], table_rows)
    counts = counts_t.T
    inverse = 1.0 / jnp.sum(counts, axis=1, keepdims=True)
    counts = counts.astype(BF)
    own_sum[...] = dot(counts[:, :node_dev], features)
    counts_bnd = counts[:, node_dev:]

    loads[6].wait()
    own_proj[...] = dot(features, ws[...])

    loads[3].wait()
    a_row = jnp.concatenate([anch[v : v + 1, :] for v in range(peers)], axis=1)
    anchors_t = marks(a_row, node_dev)
    anchors_n = anchors_t.T.astype(BF)
    anchors_t = anchors_t.astype(BF)

    loads[7].wait()

    @pl.when(has_prev)
    def _():
        up.wait_recv()

    @pl.when(has_next)
    def _():
        down.wait_recv()

    received = b_recv[...].reshape(2 * bnd_rows, width)
    mean = ((own_sum[...] + dot(counts_bnd, received)) * inverse).astype(BF)
    embed = (own_proj[...] + dot(mean, wn[...])).astype(BF)
    embed_v[...] = embed

    a_send[...] = dot(anchors_n, embed).astype(BF).reshape(peers, anch_n, width)

    def exchange(source, target, send, recv):
        return [
            pltpu.make_async_remote_copy(
                src_ref=source.at[partner[o]],
                dst_ref=target.at[w],
                send_sem=send.at[o - 1],
                recv_sem=recv.at[o - 1],
                device_id=(d, partner[o]),
                device_id_type=MESH,
            )
            for o in range(1, n_wide)
        ]

    out = exchange(a_send, a_recv, as_sem, ar_sem)
    for copy in out:
        copy.start()
    a_recv[pl.ds(w, 1)] = a_send[pl.ds(w, 1)]

    loads[4].wait()
    n_rows = jnp.concatenate([neg[v] for v in range(peers)], axis=1)
    mult_t = marks(n_rows[0:1, :], node_dev)
    for k in range(1, fan):
        mult_t = mult_t + marks(n_rows[k : k + 1, :], node_dev)
    mult = mult_t.T

    loads[5].wait()
    first = marks(pos[0:1, :], node_dev).astype(BF)
    second = marks(pos[1:2, :], node_dev).astype(BF)
    pairs = dot_nt(
        jnp.concatenate([first, second], axis=1), jnp.concatenate([second, first], axis=1)
    )

    for copy in out:
        copy.wait_recv()
    got = a_recv[...].reshape(peers * anch_n, width)
    coef = (mult * jax.nn.sigmoid(dot_nt(got, embed) * scale)).astype(BF)
    t_send[...] = dot(coef, embed).astype(BF).reshape(peers, anch_n, width)
    back = exchange(t_send, t_recv, ts_sem, tr_sem)
    for copy in back:
        copy.start()
    t_recv[pl.ds(w, 1)] = t_send[pl.ds(w, 1)]
    c_pos = pairs * (jax.nn.sigmoid(dot_nt(embed, embed) * scale) - 1.0)
    own_sum[...] = dot(c_pos.astype(BF), embed)
    own_sum[...] += dot_tn(coef, got)
    for copy in back:
        copy.wait_recv()
    terms = t_recv[...].reshape(peers * anch_n, width)
    grad_v[...] = (own_sum[...] + dot(anchors_t, terms)).astype(BF)

    @pl.when(has_next)
    def _():
        up.wait_send()

    @pl.when(has_prev)
    def _():
        down.wait_send()

    for copy in out + back:
        copy.wait_send()


def store_kernel(embed_v, grad_v, embed_out, grad_out, sem):
    stores = [
        pltpu.make_async_copy(embed_v, embed_out, sem.at[0]),
        pltpu.make_async_copy(grad_v, grad_out, sem.at[1]),
    ]
    for store in stores:
        store.start()
    for store in stores:
        store.wait()


def body(n_dom, n_wide, features, w_self, w_neigh, boundary, neighbors, anchors, negatives, positives):
    node_dev, width = features.shape
    bnd_rows = boundary.shape[2]
    peers, anch_n = anchors.shape
    small = [boundary, neighbors.T, anchors, negatives.transpose(0, 2, 1), positives.T]
    block = (peers, anch_n, width)
    far = pl.BlockSpec(memory_space=pltpu.HBM)
    near = pl.BlockSpec(memory_space=pltpu.VMEM)
    results = [jax.ShapeDtypeStruct((node_dev, width), BF)] * 2
    held = pl.pallas_call(
        functools.partial(kernel, n_dom, n_wide),
        out_shape=[pltpu.VMEM((node_dev, width), BF)] * 2,
        in_specs=[far] * 8,
        out_specs=[near] * 2,
        scratch_shapes=[
            pltpu.VMEM(features.shape, BF),
            pltpu.VMEM(w_self.shape, BF),
            pltpu.VMEM(w_neigh.shape, BF),
        ]
        + [pltpu.VMEM(x.shape, jnp.int32) for x in small]
        + [pltpu.VMEM((2, bnd_rows, width), BF)] * 2
        + [pltpu.VMEM(block, BF)] * 4
        + [pltpu.VMEM((node_dev, width), F32)] * 2
        + [
            pltpu.SemaphoreType.DMA((8,)),
            pltpu.SemaphoreType.DMA((2,)),
            pltpu.SemaphoreType.DMA((2,)),
        ]
        + [pltpu.SemaphoreType.DMA((n_wide - 1,))] * 4,
        compiler_params=pltpu.CompilerParams(
            collective_id=0, has_side_effects=True, vmem_limit_bytes=32 * 1024 * 1024
        ),
    )(*[pltpu.with_memory_space_constraint(x, pltpu.HBM) for x in (features, w_self, w_neigh, *small)])
    return pl.pallas_call(
        store_kernel,
        out_shape=results,
        in_specs=[near] * 2,
        out_specs=[far] * 2,
        scratch_shapes=[pltpu.SemaphoreType.DMA((2,))],
    )(*held)


def solution(mesh):
    return jax.shard_map(
        functools.partial(body, mesh.shape["dom"], mesh.shape["wide"]),
        mesh=mesh,
        in_specs=(
            P(("dom", "wide"), None),
            P(),
            P(),
            P(("dom", "wide"), None, None),
            P(("dom", "wide"), None),
            P(("dom", "wide"), None),
            P(("dom", "wide"), None, None),
            P(("dom", "wide"), None),
        ),
        out_specs=(P(("dom", "wide"), None), P(("dom", "wide"), None)),
        check_vma=False,
    )
```

```python
import functools
import math

import jax
import jax.numpy as jnp
from jax import lax
from jax.experimental import pallas as pl
from jax.experimental.pallas import tpu as pltpu
from jax.sharding import PartitionSpec as P

MESH = pl.DeviceIdType.MESH
BF = jnp.bfloat16
F32 = jnp.float32


def dot(a, b):
    return jnp.dot(a, b, preferred_element_type=F32)


def dot_nt(a, b):
    return lax.dot_general(a, b, (((1,), (1,)), ((), ())), preferred_element_type=F32)


def dot_tn(a, b):
    return lax.dot_general(a, b, (((0,), (0,)), ((), ())), preferred_element_type=F32)


def marks(row, height):
    rows = lax.broadcasted_iota(jnp.int32, (height, row.shape[1]), 0)
    return jnp.where(rows == row, 1.0, 0.0)


def peer_at(w, o, n):
    if n & (n - 1):
        return lax.rem(w + o + n, n)
    bit = 1
    while bit <= o:
        if o & bit:
            w = w + bit * (1 - 2 * lax.rem(w // bit, 2))
        bit *= 2
    return w


def kernel(
    n_dom,
    n_wide,
    feat_in,
    ws_in,
    wn_in,
    bnd_in,
    nbr_in,
    anch_in,
    neg_in,
    pos_in,
    embed_v,
    grad_v,
    feat,
    ws,
    wn,
    bnd,
    nbr,
    anch,
    neg,
    pos,
    b_send,
    b_recv,
    a_send,
    a_recv,
    t_send,
    t_recv,
    mult,
    coef,
    own_sum,
    own_proj,
    load_sem,
    bs_sem,
    br_sem,
    as_sem,
    ar_sem,
    ts_sem,
    tr_sem,
):
    node_dev, width = feat.shape
    slots = nbr.shape[0]
    bnd_rows = bnd.shape[2]
    peers, anch_n = anch.shape
    fan = neg.shape[1]
    scale = 1.0 / math.sqrt(width)
    d = lax.axis_index("dom")
    w = lax.axis_index("wide")
    has_prev = d > 0
    has_next = d < n_dom - 1

    loads = [
        pltpu.make_async_copy(src, dst, load_sem.at[i])
        for i, (src, dst) in enumerate(
            [
                (bnd_in, bnd),
                (feat_in, feat),
                (nbr_in, nbr),
                (anch_in, anch),
                (neg_in, neg),
                (pos_in, pos),
                (ws_in, ws),
                (wn_in, wn),
            ]
        )
    ]
    for load in loads:
        load.start()

    barrier = pltpu.get_barrier_semaphore()

    @pl.when(has_prev)
    def _():
        pl.semaphore_signal(barrier, inc=1, device_id=(d - 1, w), device_id_type=MESH)

    @pl.when(has_next)
    def _():
        pl.semaphore_signal(barrier, inc=1, device_id=(d + 1, w), device_id_type=MESH)

    partner = [peer_at(w, o, n_wide) for o in range(n_wide)]
    origin = partner if n_wide & (n_wide - 1) == 0 else [peer_at(w, -o, n_wide) for o in range(n_wide)]
    for o in range(1, n_wide):
        pl.semaphore_signal(barrier, inc=1, device_id=(d, partner[o]), device_id_type=MESH)

    loads[0].wait()
    loads[1].wait()
    features = feat[...]
    b_row = jnp.concatenate([bnd[0, 0:1, :], bnd[0, 1:2, :]], axis=1)
    picked = dot_tn(marks(b_row, node_dev).astype(BF), features)
    b_send[...] = picked.astype(BF).reshape(2, bnd_rows, width)

    arrivals = n_wide - 1 + has_prev.astype(jnp.int32) + has_next.astype(jnp.int32)
    pl.semaphore_wait(barrier, arrivals)

    up = pltpu.make_async_remote_copy(
        src_ref=b_send.at[0],
        dst_ref=b_recv.at[0],
        send_sem=bs_sem.at[0],
        recv_sem=br_sem.at[0],
        device_id=(d + 1, w),
        device_id_type=MESH,
    )
    down = pltpu.make_async_remote_copy(
        src_ref=b_send.at[1],
        dst_ref=b_recv.at[1],
        send_sem=bs_sem.at[1],
        recv_sem=br_sem.at[1],
        device_id=(d - 1, w),
        device_id_type=MESH,
    )

    @pl.when(has_next)
    def _():
        up.start()

    @pl.when(has_prev)
    def _():
        down.start()

    @pl.when(jnp.logical_not(has_prev))
    def _():
        b_recv[0] = jnp.zeros((bnd_rows, width), BF)

    @pl.when(jnp.logical_not(has_next))
    def _():
        b_recv[1] = jnp.zeros((bnd_rows, width), BF)

    loads[2].wait()
    table_rows = node_dev + 2 * bnd_rows
    counts_t = marks(nbr[0:1, :], table_rows)
    for slot in range(1, slots):
        counts_t = counts_t + marks(nbr[slot : slot + 1, :], table_rows)
    counts = counts_t.T.astype(BF)

    loads[3].wait()
    a_row = jnp.concatenate([anch[v : v + 1, :] for v in range(peers)], axis=1)
    anchors_t = marks(a_row, node_dev)
    anchors_n = anchors_t.T.astype(BF)
    anchors_t = anchors_t.astype(BF)
    n_anch = peers * anch_n
    picked_counts = dot(anchors_n, counts)
    counts_a = picked_counts.astype(BF)
    inverse_a = 1.0 / jnp.sum(picked_counts, axis=1, keepdims=True)
    inverse = 1.0 / jnp.sum(counts.astype(F32), axis=1, keepdims=True)
    both = jnp.concatenate([counts_a[:, :node_dev], counts[:, :node_dev]], axis=0)
    own_sum[...] = dot(both, features)

    loads[6].wait()
    feat_a = dot(anchors_n, features).astype(BF)
    own_proj[...] = dot(jnp.concatenate([feat_a, features], axis=0), ws[...])

    loads[4].wait()
    n_rows = jnp.concatenate([neg[v] for v in range(peers)], axis=1)
    mult_t = marks(n_rows[0:1, :], node_dev)
    for k in range(1, fan):
        mult_t = mult_t + marks(n_rows[k : k + 1, :], node_dev)
    mult[...] = mult_t.T.reshape(peers, anch_n, node_dev)
    loads[7].wait()

    @pl.when(has_prev)
    def _():
        up.wait_recv()

    @pl.when(has_next)
    def _():
        down.wait_recv()

    received = b_recv[...].reshape(2 * bnd_rows, width)

    def embedding(rows, bnd_counts, inv):
        mean = ((own_sum[rows, :] + dot(bnd_counts, received)) * inv).astype(BF)
        return (own_proj[rows, :] + dot(mean, wn[...])).astype(BF)

    anchor_embed = embedding(pl.ds(0, n_anch), counts_a[:, node_dev:], inverse_a)
    a_send[...] = anchor_embed.reshape(peers, anch_n, width)

    def exchange(source, target, send, recv, to):
        return [
            pltpu.make_async_remote_copy(
                src_ref=source.at[to[o]],
                dst_ref=target.at[w],
                send_sem=send.at[o - 1],
                recv_sem=recv.at[o - 1],
                device_id=(d, to[o]),
                device_id_type=MESH,
            )
            for o in range(1, n_wide)
        ]

    out = exchange(a_send, a_recv, as_sem, ar_sem, partner)
    for copy in out[1:] + out[:1]:
        copy.start()
    a_recv[pl.ds(w, 1)] = a_send[pl.ds(w, 1)]

    embed = embedding(pl.ds(n_anch, node_dev), counts[:, node_dev:], inverse)
    embed_v[...] = embed

    loads[5].wait()
    first = marks(pos[0:1, :], node_dev).astype(BF)
    second = marks(pos[1:2, :], node_dev).astype(BF)
    pairs = dot_nt(
        jnp.concatenate([first, second], axis=1), jnp.concatenate([second, first], axis=1)
    )

    back = exchange(t_send, t_recv, ts_sem, tr_sem, origin)

    def answer(v):
        score = dot_nt(a_recv[v], embed) * scale
        c = (mult[v] * jax.nn.sigmoid(score)).astype(BF)
        coef[v] = c
        return dot(c, embed).astype(BF)

    t_recv[w] = answer(w)
    for copy, reply, v in zip(out, back, origin[1:]):
        copy.wait_recv()
        t_send[v] = answer(v)
        reply.start()

    c_pos = pairs * (jax.nn.sigmoid(dot_nt(embed, embed) * scale) - 1.0)
    got = a_recv[...].reshape(n_anch, width)
    grad = dot(c_pos.astype(BF), embed) + dot_tn(coef[...].reshape(n_anch, node_dev), got)
    for copy in back:
        copy.wait_recv()
    terms = t_recv[...].reshape(n_anch, width)
    grad_v[...] = (grad + dot(anchors_t, terms)).astype(BF)

    @pl.when(has_next)
    def _():
        up.wait_send()

    @pl.when(has_prev)
    def _():
        down.wait_send()

    for copy in out + back:
        copy.wait_send()


def store_kernel(embed_v, grad_v, embed_out, grad_out, sem):
    stores = [
        pltpu.make_async_copy(embed_v, embed_out, sem.at[0]),
        pltpu.make_async_copy(grad_v, grad_out, sem.at[1]),
    ]
    for store in stores:
        store.start()
    for store in stores:
        store.wait()


def body(n_dom, n_wide, features, w_self, w_neigh, boundary, neighbors, anchors, negatives, positives):
    node_dev, width = features.shape
    bnd_rows = boundary.shape[2]
    peers, anch_n = anchors.shape
    small = [boundary, neighbors.T, anchors, negatives.transpose(0, 2, 1), positives.T]
    block = (peers, anch_n, width)
    far = pl.BlockSpec(memory_space=pltpu.HBM)
    near = pl.BlockSpec(memory_space=pltpu.VMEM)
    results = [jax.ShapeDtypeStruct((node_dev, width), BF)] * 2
    held = pl.pallas_call(
        functools.partial(kernel, n_dom, n_wide),
        out_shape=[pltpu.VMEM((node_dev, width), BF)] * 2,
        in_specs=[far] * 8,
        out_specs=[near] * 2,
        scratch_shapes=[
            pltpu.VMEM(features.shape, BF),
            pltpu.VMEM(w_self.shape, BF),
            pltpu.VMEM(w_neigh.shape, BF),
        ]
        + [pltpu.VMEM(x.shape, jnp.int32) for x in small]
        + [pltpu.VMEM((2, bnd_rows, width), BF)] * 2
        + [pltpu.VMEM(block, BF)] * 4
        + [
            pltpu.VMEM((peers, anch_n, node_dev), F32),
            pltpu.VMEM((peers, anch_n, node_dev), BF),
        ]
        + [pltpu.VMEM((peers * anch_n + node_dev, width), F32)] * 2
        + [
            pltpu.SemaphoreType.DMA((8,)),
            pltpu.SemaphoreType.DMA((2,)),
            pltpu.SemaphoreType.DMA((2,)),
        ]
        + [pltpu.SemaphoreType.DMA((n_wide - 1,))] * 4,
        compiler_params=pltpu.CompilerParams(
            collective_id=0, has_side_effects=True, vmem_limit_bytes=32 * 1024 * 1024
        ),
    )(*[pltpu.with_memory_space_constraint(x, pltpu.HBM) for x in (features, w_self, w_neigh, *small)])
    return pl.pallas_call(
        store_kernel,
        out_shape=results,
        in_specs=[near] * 2,
        out_specs=[far] * 2,
        scratch_shapes=[pltpu.SemaphoreType.DMA((2,))],
        compiler_params=pltpu.CompilerParams(vmem_limit_bytes=4 * 1024 * 1024),
    )(*[pltpu.with_memory_space_constraint(x, pltpu.VMEM) for x in held])


def solution(mesh):
    return jax.shard_map(
        functools.partial(body, mesh.shape["dom"], mesh.shape["wide"]),
        mesh=mesh,
        in_specs=(
            P(("dom", "wide"), None),
            P(),
            P(),
            P(("dom", "wide"), None, None),
            P(("dom", "wide"), None),
            P(("dom", "wide"), None),
            P(("dom", "wide"), None, None),
            P(("dom", "wide"), None),
        ),
        out_specs=(P(("dom", "wide"), None), P(("dom", "wide"), None)),
        check_vma=False,
    )
```

```python
import functools
import math

import jax
import jax.numpy as jnp
from jax import lax
from jax.experimental import pallas as pl
from jax.experimental.pallas import tpu as pltpu
from jax.sharding import PartitionSpec as P

MESH = pl.DeviceIdType.MESH
BF = jnp.bfloat16
F32 = jnp.float32


def dot(a, b):
    return jnp.dot(a, b, preferred_element_type=F32)


def dot_nt(a, b):
    return lax.dot_general(a, b, (((1,), (1,)), ((), ())), preferred_element_type=F32)


def dot_tn(a, b):
    return lax.dot_general(a, b, (((0,), (0,)), ((), ())), preferred_element_type=F32)


def marks(row, height):
    rows = lax.broadcasted_iota(jnp.int32, (height, row.shape[1]), 0)
    return jnp.where(rows == row, 1.0, 0.0)


def peer_at(w, o, n):
    if n & (n - 1):
        return lax.rem(w + o + n, n)
    bit = 1
    while bit <= o:
        if o & bit:
            w = w + bit * (1 - 2 * lax.rem(w // bit, 2))
        bit *= 2
    return w


def kernel(
    n_dom,
    n_wide,
    feat_in,
    ws_in,
    wn_in,
    bnd_in,
    nbr_in,
    anch_in,
    neg_in,
    pos_in,
    embed_v,
    grad_v,
    feat,
    ws,
    wn,
    bnd,
    nbr,
    anch,
    neg,
    pos,
    b_send,
    b_recv,
    a_send,
    a_recv,
    t_send,
    t_recv,
    mult,
    coef,
    own_sum,
    own_proj,
    load_sem,
    bs_sem,
    br_sem,
    as_sem,
    ar_sem,
    ts_sem,
    tr_sem,
):
    node_dev, width = feat.shape
    slots = nbr.shape[0]
    bnd_rows = bnd.shape[2]
    peers, anch_n = anch.shape
    fan = neg.shape[1]
    scale = 1.0 / math.sqrt(width)
    d = lax.axis_index("dom")
    w = lax.axis_index("wide")
    has_prev = d > 0
    has_next = d < n_dom - 1

    loads = [
        pltpu.make_async_copy(src, dst, load_sem.at[i])
        for i, (src, dst) in enumerate(
            [
                (bnd_in, bnd),
                (feat_in, feat),
                (nbr_in, nbr),
                (anch_in, anch),
                (neg_in, neg),
                (pos_in, pos),
                (ws_in, ws),
                (wn_in, wn),
            ]
        )
    ]
    for load in loads[:2]:
        load.start()

    barrier = pltpu.get_barrier_semaphore()

    @pl.when(has_prev)
    def _():
        pl.semaphore_signal(barrier, inc=1, device_id=(d - 1, w), device_id_type=MESH)

    @pl.when(has_next)
    def _():
        pl.semaphore_signal(barrier, inc=1, device_id=(d + 1, w), device_id_type=MESH)

    partner = [peer_at(w, o, n_wide) for o in range(n_wide)]
    origin = partner if n_wide & (n_wide - 1) == 0 else [peer_at(w, -o, n_wide) for o in range(n_wide)]
    for o in range(1, n_wide):
        pl.semaphore_signal(barrier, inc=1, device_id=(d, partner[o]), device_id_type=MESH)

    loads[0].wait()
    b_row = jnp.concatenate([bnd[0, 0:1, :], bnd[0, 1:2, :]], axis=1)
    b_pick = marks(b_row, node_dev).T.astype(BF)
    loads[1].wait()
    for load in loads[2:]:
        load.start()
    features = feat[...]
    picked = dot(b_pick, features)
    b_send[...] = picked.astype(BF).reshape(2, bnd_rows, width)

    arrivals = n_wide - 1 + has_prev.astype(jnp.int32) + has_next.astype(jnp.int32)
    pl.semaphore_wait(barrier, arrivals)

    up = pltpu.make_async_remote_copy(
        src_ref=b_send.at[0],
        dst_ref=b_recv.at[0],
        send_sem=bs_sem.at[0],
        recv_sem=br_sem.at[0],
        device_id=(d + 1, w),
        device_id_type=MESH,
    )
    down = pltpu.make_async_remote_copy(
        src_ref=b_send.at[1],
        dst_ref=b_recv.at[1],
        send_sem=bs_sem.at[1],
        recv_sem=br_sem.at[1],
        device_id=(d - 1, w),
        device_id_type=MESH,
    )

    @pl.when(has_next)
    def _():
        up.start()

    @pl.when(has_prev)
    def _():
        down.start()

    @pl.when(jnp.logical_not(has_prev))
    def _():
        b_recv[0] = jnp.zeros((bnd_rows, width), BF)

    @pl.when(jnp.logical_not(has_next))
    def _():
        b_recv[1] = jnp.zeros((bnd_rows, width), BF)

    loads[2].wait()
    table_rows = node_dev + 2 * bnd_rows
    counts_t = marks(nbr[0:1, :], table_rows)
    for slot in range(1, slots):
        counts_t = counts_t + marks(nbr[slot : slot + 1, :], table_rows)
    counts = counts_t.T.astype(BF)

    loads[3].wait()
    a_row = jnp.concatenate([anch[v : v + 1, :] for v in range(peers)], axis=1)
    anchors_t = marks(a_row, node_dev)
    anchors_n = anchors_t.T.astype(BF)
    anchors_t = anchors_t.astype(BF)
    n_anch = peers * anch_n
    picked_counts = dot(anchors_n, counts)
    counts_a = picked_counts.astype(BF)
    inverse_a = 1.0 / jnp.sum(picked_counts, axis=1, keepdims=True)
    inverse = 1.0 / jnp.sum(counts.astype(F32), axis=1, keepdims=True)
    both = jnp.concatenate([counts_a[:, :node_dev], counts[:, :node_dev]], axis=0)
    own_sum[...] = dot(both, features)

    loads[6].wait()
    feat_a = dot(anchors_n, features).astype(BF)
    own_proj[...] = dot(jnp.concatenate([feat_a, features], axis=0), ws[...])

    loads[4].wait()
    n_rows = jnp.concatenate([neg[v] for v in range(peers)], axis=1)
    mult_t = marks(n_rows[0:1, :], node_dev)
    for k in range(1, fan):
        mult_t = mult_t + marks(n_rows[k : k + 1, :], node_dev)
    mult[...] = mult_t.T.reshape(peers, anch_n, node_dev)
    loads[7].wait()

    @pl.when(has_prev)
    def _():
        up.wait_recv()

    @pl.when(has_next)
    def _():
        down.wait_recv()

    received = b_recv[...].reshape(2 * bnd_rows, width)

    def embedding(rows, bnd_counts, inv):
        mean = ((own_sum[rows, :] + dot(bnd_counts, received)) * inv).astype(BF)
        return (own_proj[rows, :] + dot(mean, wn[...])).astype(BF)

    anchor_embed = embedding(pl.ds(0, n_anch), counts_a[:, node_dev:], inverse_a)
    a_send[...] = anchor_embed.reshape(peers, anch_n, width)

    def exchange(source, target, send, recv, to):
        return [
            pltpu.make_async_remote_copy(
                src_ref=source.at[to[o]],
                dst_ref=target.at[w],
                send_sem=send.at[o - 1],
                recv_sem=recv.at[o - 1],
                device_id=(d, to[o]),
                device_id_type=MESH,
            )
            for o in range(1, n_wide)
        ]

    out = exchange(a_send, a_recv, as_sem, ar_sem, partner)
    for copy in out[1:] + out[:1]:
        copy.start()
    a_recv[pl.ds(w, 1)] = a_send[pl.ds(w, 1)]

    embed = embedding(pl.ds(n_anch, node_dev), counts[:, node_dev:], inverse)
    embed_v[...] = embed

    back = exchange(t_send, t_recv, ts_sem, tr_sem, origin)

    def answer(v):
        score = dot_nt(a_recv[v], embed) * scale
        c = (mult[v] * jax.nn.sigmoid(score)).astype(BF)
        coef[v] = c
        return dot(c, embed).astype(BF)

    for copy, reply, v in zip(out, back, origin[1:]):
        copy.wait_recv()
        t_send[v] = answer(v)
        reply.start()

    loads[5].wait()
    first = marks(pos[0:1, :], node_dev).astype(BF)
    second = marks(pos[1:2, :], node_dev).astype(BF)
    pairs = dot_nt(
        jnp.concatenate([first, second], axis=1), jnp.concatenate([second, first], axis=1)
    )
    t_recv[w] = answer(w)
    c_pos = pairs * (jax.nn.sigmoid(dot_nt(embed, embed) * scale) - 1.0)
    got = a_recv[...].reshape(n_anch, width)
    grad = dot(c_pos.astype(BF), embed) + dot_tn(coef[...].reshape(n_anch, node_dev), got)
    for copy in back:
        copy.wait_recv()
    terms = t_recv[...].reshape(n_anch, width)
    grad_v[...] = (grad + dot(anchors_t, terms)).astype(BF)

    @pl.when(has_next)
    def _():
        up.wait_send()

    @pl.when(has_prev)
    def _():
        down.wait_send()

    for copy in out + back:
        copy.wait_send()


def store_kernel(embed_v, grad_v, embed_out, grad_out, sem):
    stores = [
        pltpu.make_async_copy(embed_v, embed_out, sem.at[0]),
        pltpu.make_async_copy(grad_v, grad_out, sem.at[1]),
    ]
    for store in stores:
        store.start()
    for store in stores:
        store.wait()


def body(n_dom, n_wide, features, w_self, w_neigh, boundary, neighbors, anchors, negatives, positives):
    node_dev, width = features.shape
    bnd_rows = boundary.shape[2]
    peers, anch_n = anchors.shape
    small = [boundary, neighbors.T, anchors, negatives.transpose(0, 2, 1), positives.T]
    block = (peers, anch_n, width)
    far = pl.BlockSpec(memory_space=pltpu.HBM)
    near = pl.BlockSpec(memory_space=pltpu.VMEM)
    results = [jax.ShapeDtypeStruct((node_dev, width), BF)] * 2
    held = pl.pallas_call(
        functools.partial(kernel, n_dom, n_wide),
        out_shape=[pltpu.VMEM((node_dev, width), BF)] * 2,
        in_specs=[far] * 8,
        out_specs=[near] * 2,
        scratch_shapes=[
            pltpu.VMEM(features.shape, BF),
            pltpu.VMEM(w_self.shape, BF),
            pltpu.VMEM(w_neigh.shape, BF),
        ]
        + [pltpu.VMEM(x.shape, jnp.int32) for x in small]
        + [pltpu.VMEM((2, bnd_rows, width), BF)] * 2
        + [pltpu.VMEM(block, BF)] * 4
        + [
            pltpu.VMEM((peers, anch_n, node_dev), F32),
            pltpu.VMEM((peers, anch_n, node_dev), BF),
        ]
        + [pltpu.VMEM((peers * anch_n + node_dev, width), F32)] * 2
        + [
            pltpu.SemaphoreType.DMA((8,)),
            pltpu.SemaphoreType.DMA((2,)),
            pltpu.SemaphoreType.DMA((2,)),
        ]
        + [pltpu.SemaphoreType.DMA((n_wide - 1,))] * 4,
        compiler_params=pltpu.CompilerParams(
            collective_id=0, has_side_effects=True, vmem_limit_bytes=32 * 1024 * 1024
        ),
    )(*[pltpu.with_memory_space_constraint(x, pltpu.HBM) for x in (features, w_self, w_neigh, *small)])
    return pl.pallas_call(
        store_kernel,
        out_shape=results,
        in_specs=[near] * 2,
        out_specs=[far] * 2,
        scratch_shapes=[pltpu.SemaphoreType.DMA((2,))],
        compiler_params=pltpu.CompilerParams(vmem_limit_bytes=4 * 1024 * 1024),
    )(*[pltpu.with_memory_space_constraint(x, pltpu.VMEM) for x in held])


def solution(mesh):
    return jax.shard_map(
        functools.partial(body, mesh.shape["dom"], mesh.shape["wide"]),
        mesh=mesh,
        in_specs=(
            P(("dom", "wide"), None),
            P(),
            P(),
            P(("dom", "wide"), None, None),
            P(("dom", "wide"), None),
            P(("dom", "wide"), None),
            P(("dom", "wide"), None, None),
            P(("dom", "wide"), None),
        ),
        out_specs=(P(("dom", "wide"), None), P(("dom", "wide"), None)),
        check_vma=False,
    )
```

```python
import functools
import math

import jax
import jax.numpy as jnp
from jax import lax
from jax.experimental import pallas as pl
from jax.experimental.pallas import tpu as pltpu
from jax.sharding import PartitionSpec as P

MESH = pl.DeviceIdType.MESH
BF = jnp.bfloat16
F32 = jnp.float32


def dot(a, b):
    return jnp.dot(a, b, preferred_element_type=F32)


def dot_nt(a, b):
    return lax.dot_general(a, b, (((1,), (1,)), ((), ())), preferred_element_type=F32)


def dot_tn(a, b):
    return lax.dot_general(a, b, (((0,), (0,)), ((), ())), preferred_element_type=F32)


def marks(row, height):
    rows = lax.broadcasted_iota(jnp.int32, (height, row.shape[1]), 0)
    return jnp.where(rows == row, 1.0, 0.0)


def peer_at(w, o, n):
    if n & (n - 1):
        return lax.rem(w + o + n, n)
    bit = 1
    while bit <= o:
        if o & bit:
            w = w + bit * (1 - 2 * lax.rem(w // bit, 2))
        bit *= 2
    return w


def kernel(
    n_dom,
    n_wide,
    feat_in,
    ws_in,
    wn_in,
    bnd_in,
    nbr_in,
    anch_in,
    neg_in,
    pos_in,
    embed_v,
    grad_v,
    feat,
    ws,
    wn,
    bnd,
    nbr,
    anch,
    neg,
    pos,
    b_send,
    b_recv,
    a_send,
    a_recv,
    t_send,
    t_recv,
    mult,
    coef,
    embed_t,
    own_sum,
    own_proj,
    load_sem,
    bs_sem,
    br_sem,
    as_sem,
    ar_sem,
    ts_sem,
    tr_sem,
):
    node_dev, width = feat.shape
    slots = nbr.shape[0]
    bnd_rows = bnd.shape[2]
    peers, anch_n = anch.shape
    fan = neg.shape[1]
    scale = 1.0 / math.sqrt(width)
    d = lax.axis_index("dom")
    w = lax.axis_index("wide")
    has_prev = d > 0
    has_next = d < n_dom - 1

    loads = [
        pltpu.make_async_copy(src, dst, load_sem.at[i])
        for i, (src, dst) in enumerate(
            [
                (bnd_in, bnd),
                (feat_in, feat),
                (nbr_in, nbr),
                (anch_in, anch),
                (neg_in, neg),
                (pos_in, pos),
                (ws_in, ws),
                (wn_in, wn),
            ]
        )
    ]
    for load in loads[:2]:
        load.start()

    barrier = pltpu.get_barrier_semaphore()

    @pl.when(has_prev)
    def _():
        pl.semaphore_signal(barrier, inc=1, device_id=(d - 1, w), device_id_type=MESH)

    @pl.when(has_next)
    def _():
        pl.semaphore_signal(barrier, inc=1, device_id=(d + 1, w), device_id_type=MESH)

    partner = [peer_at(w, o, n_wide) for o in range(n_wide)]
    origin = partner if n_wide & (n_wide - 1) == 0 else [peer_at(w, -o, n_wide) for o in range(n_wide)]
    for o in range(1, n_wide):
        pl.semaphore_signal(barrier, inc=1, device_id=(d, partner[o]), device_id_type=MESH)

    loads[0].wait()
    b_row = jnp.concatenate([bnd[0, 0:1, :], bnd[0, 1:2, :]], axis=1)
    b_pick = marks(b_row, node_dev).T.astype(BF)
    loads[1].wait()
    for load in loads[2:]:
        load.start()
    features = feat[...]
    picked = dot(b_pick, features)
    b_send[...] = picked.astype(BF).reshape(2, bnd_rows, width)

    arrivals = n_wide - 1 + has_prev.astype(jnp.int32) + has_next.astype(jnp.int32)
    pl.semaphore_wait(barrier, arrivals)

    up = pltpu.make_async_remote_copy(
        src_ref=b_send.at[0],
        dst_ref=b_recv.at[0],
        send_sem=bs_sem.at[0],
        recv_sem=br_sem.at[0],
        device_id=(d + 1, w),
        device_id_type=MESH,
    )
    down = pltpu.make_async_remote_copy(
        src_ref=b_send.at[1],
        dst_ref=b_recv.at[1],
        send_sem=bs_sem.at[1],
        recv_sem=br_sem.at[1],
        device_id=(d - 1, w),
        device_id_type=MESH,
    )

    even = lax.rem(d, 2) == 0

    @pl.when(jnp.logical_and(has_prev, even))
    def _():
        down.start()

    @pl.when(has_next)
    def _():
        up.start()

    @pl.when(jnp.logical_and(has_prev, jnp.logical_not(even)))
    def _():
        down.start()

    @pl.when(jnp.logical_not(has_prev))
    def _():
        b_recv[0] = jnp.zeros((bnd_rows, width), BF)

    @pl.when(jnp.logical_not(has_next))
    def _():
        b_recv[1] = jnp.zeros((bnd_rows, width), BF)

    loads[2].wait()
    table_rows = node_dev + 2 * bnd_rows
    counts_t = marks(nbr[0:1, :], table_rows)
    for slot in range(1, slots):
        counts_t = counts_t + marks(nbr[slot : slot + 1, :], table_rows)
    counts = counts_t.T.astype(BF)

    loads[3].wait()
    a_row = jnp.concatenate([anch[v : v + 1, :] for v in range(peers)], axis=1)
    anchors_t = marks(a_row, node_dev)
    anchors_n = anchors_t.T.astype(BF)
    anchors_t = anchors_t.astype(BF)
    n_anch = peers * anch_n
    picked_counts = dot(anchors_n, counts)
    counts_a = picked_counts.astype(BF)
    inverse_a = 1.0 / jnp.sum(picked_counts, axis=1, keepdims=True)
    inverse = 1.0 / jnp.sum(counts.astype(F32), axis=1, keepdims=True)
    both = jnp.concatenate([counts_a[:, :node_dev], counts[:, :node_dev]], axis=0)
    own_sum[...] = dot(both, features)

    loads[6].wait()
    feat_a = dot(anchors_n, features).astype(BF)
    own_proj[...] = dot(jnp.concatenate([feat_a, features], axis=0), ws[...])

    loads[4].wait()
    n_rows = jnp.concatenate([neg[v] for v in range(peers)], axis=1)
    mult_t = marks(n_rows[0:1, :], node_dev)
    for k in range(1, fan):
        mult_t = mult_t + marks(n_rows[k : k + 1, :], node_dev)
    mult[...] = mult_t.T.reshape(peers, anch_n, node_dev)
    loads[7].wait()

    @pl.when(has_prev)
    def _():
        up.wait_recv()

    @pl.when(has_next)
    def _():
        down.wait_recv()

    received = b_recv[...].reshape(2 * bnd_rows, width)

    def embedding(rows, bnd_counts, inv):
        mean = ((own_sum[rows, :] + dot(bnd_counts, received)) * inv).astype(BF)
        return (own_proj[rows, :] + dot(mean, wn[...])).astype(BF)

    anchor_embed = embedding(pl.ds(0, n_anch), counts_a[:, node_dev:], inverse_a)
    a_send[...] = anchor_embed.reshape(peers, anch_n, width)

    def exchange(source, target, send, recv, to):
        return [
            pltpu.make_async_remote_copy(
                src_ref=source.at[to[o]],
                dst_ref=target.at[w],
                send_sem=send.at[o - 1],
                recv_sem=recv.at[o - 1],
                device_id=(d, to[o]),
                device_id_type=MESH,
            )
            for o in range(1, n_wide)
        ]

    out = exchange(a_send, a_recv, as_sem, ar_sem, partner)
    for copy in out:
        copy.start()
    a_recv[pl.ds(w, 1)] = a_send[pl.ds(w, 1)]

    embed = embedding(pl.ds(n_anch, node_dev), counts[:, node_dev:], inverse)
    embed_v[...] = embed
    embed_t[...] = embed.T

    back = exchange(t_send, t_recv, ts_sem, tr_sem, origin)

    def answer(v):
        score = dot(a_recv[v], embed_t[...]) * scale
        c = (mult[v] * jax.nn.sigmoid(score)).astype(BF)
        coef[v] = c
        return dot(c, embed).astype(BF)

    for copy, reply, v in zip(out, back, origin[1:]):
        copy.wait_recv()
        t_send[v] = answer(v)
        reply.start()

    loads[5].wait()
    first = marks(pos[0:1, :], node_dev).astype(BF)
    second = marks(pos[1:2, :], node_dev).astype(BF)
    pairs = dot_nt(
        jnp.concatenate([first, second], axis=1), jnp.concatenate([second, first], axis=1)
    )
    t_recv[w] = answer(w)
    c_pos = pairs * (jax.nn.sigmoid(dot(embed, embed_t[...]) * scale) - 1.0)
    got = a_recv[...].reshape(n_anch, width)
    grad = dot(c_pos.astype(BF), embed) + dot_tn(coef[...].reshape(n_anch, node_dev), got)
    for copy in back:
        copy.wait_recv()
    terms = t_recv[...].reshape(n_anch, width)
    grad_v[...] = (grad + dot(anchors_t, terms)).astype(BF)

    @pl.when(has_next)
    def _():
        up.wait_send()

    @pl.when(has_prev)
    def _():
        down.wait_send()

    for copy in out + back:
        copy.wait_send()


def store_kernel(embed_v, grad_v, embed_out, grad_out, sem):
    stores = [
        pltpu.make_async_copy(embed_v, embed_out, sem.at[0]),
        pltpu.make_async_copy(grad_v, grad_out, sem.at[1]),
    ]
    for store in stores:
        store.start()
    for store in stores:
        store.wait()


def body(n_dom, n_wide, features, w_self, w_neigh, boundary, neighbors, anchors, negatives, positives):
    node_dev, width = features.shape
    bnd_rows = boundary.shape[2]
    peers, anch_n = anchors.shape
    small = [boundary, neighbors.T, anchors, negatives.transpose(0, 2, 1), positives.T]
    block = (peers, anch_n, width)
    far = pl.BlockSpec(memory_space=pltpu.HBM)
    near = pl.BlockSpec(memory_space=pltpu.VMEM)
    results = [jax.ShapeDtypeStruct((node_dev, width), BF)] * 2
    held = pl.pallas_call(
        functools.partial(kernel, n_dom, n_wide),
        out_shape=[pltpu.VMEM((node_dev, width), BF)] * 2,
        in_specs=[far] * 8,
        out_specs=[near] * 2,
        scratch_shapes=[
            pltpu.VMEM(features.shape, BF),
            pltpu.VMEM(w_self.shape, BF),
            pltpu.VMEM(w_neigh.shape, BF),
        ]
        + [pltpu.VMEM(x.shape, jnp.int32) for x in small]
        + [pltpu.VMEM((2, bnd_rows, width), BF)] * 2
        + [pltpu.VMEM(block, BF)] * 4
        + [
            pltpu.VMEM((peers, anch_n, node_dev), F32),
            pltpu.VMEM((peers, anch_n, node_dev), BF),
            pltpu.VMEM((width, node_dev), BF),
        ]
        + [pltpu.VMEM((peers * anch_n + node_dev, width), F32)] * 2
        + [
            pltpu.SemaphoreType.DMA((8,)),
            pltpu.SemaphoreType.DMA((2,)),
            pltpu.SemaphoreType.DMA((2,)),
        ]
        + [pltpu.SemaphoreType.DMA((n_wide - 1,))] * 4,
        compiler_params=pltpu.CompilerParams(
            collective_id=0, has_side_effects=True, vmem_limit_bytes=32 * 1024 * 1024
        ),
    )(*[pltpu.with_memory_space_constraint(x, pltpu.HBM) for x in (features, w_self, w_neigh, *small)])
    return pl.pallas_call(
        store_kernel,
        out_shape=results,
        in_specs=[near] * 2,
        out_specs=[far] * 2,
        scratch_shapes=[pltpu.SemaphoreType.DMA((2,))],
        compiler_params=pltpu.CompilerParams(vmem_limit_bytes=4 * 1024 * 1024),
    )(*[pltpu.with_memory_space_constraint(x, pltpu.VMEM) for x in held])


def solution(mesh):
    return jax.shard_map(
        functools.partial(body, mesh.shape["dom"], mesh.shape["wide"]),
        mesh=mesh,
        in_specs=(
            P(("dom", "wide"), None),
            P(),
            P(),
            P(("dom", "wide"), None, None),
            P(("dom", "wide"), None),
            P(("dom", "wide"), None),
            P(("dom", "wide"), None, None),
            P(("dom", "wide"), None),
        ),
        out_specs=(P(("dom", "wide"), None), P(("dom", "wide"), None)),
        check_vma=False,
    )
```

```python
import functools
import math

import jax
import jax.numpy as jnp
from jax import lax
from jax.experimental import pallas as pl
from jax.experimental.pallas import tpu as pltpu
from jax.sharding import PartitionSpec as P

MESH = pl.DeviceIdType.MESH
BF = jnp.bfloat16
F32 = jnp.float32


def dot(a, b):
    return jnp.dot(a, b, preferred_element_type=F32)


def dot_nt(a, b):
    return lax.dot_general(a, b, (((1,), (1,)), ((), ())), preferred_element_type=F32)


def dot_tn(a, b):
    return lax.dot_general(a, b, (((0,), (0,)), ((), ())), preferred_element_type=F32)


def marks(row, height):
    rows = lax.broadcasted_iota(jnp.int32, (height, row.shape[1]), 0)
    return jnp.where(rows == row, 1.0, 0.0)


def peer_at(w, o, n):
    if n & (n - 1):
        return lax.rem(w + o + n, n)
    bit = 1
    while bit <= o:
        if o & bit:
            w = w + bit * (1 - 2 * lax.rem(w // bit, 2))
        bit *= 2
    return w


def kernel(
    n_dom,
    n_wide,
    feat_in,
    ws_in,
    wn_in,
    bnd_in,
    nbr_in,
    anch_in,
    neg_in,
    pos_in,
    embed_v,
    grad_v,
    feat,
    ws,
    wn,
    bnd,
    nbr,
    anch,
    neg,
    pos,
    b_send,
    b_recv,
    a_send,
    a_recv,
    t_send,
    t_recv,
    mult,
    coef,
    embed_t,
    own_sum,
    own_proj,
    load_sem,
    bs_sem,
    br_sem,
    as_sem,
    ar_sem,
    ts_sem,
    tr_sem,
):
    node_dev, width = feat.shape
    slots = nbr.shape[0]
    bnd_rows = bnd.shape[2]
    peers, anch_n = anch.shape
    fan = neg.shape[1]
    scale = 1.0 / math.sqrt(width)
    d = lax.axis_index("dom")
    w = lax.axis_index("wide")
    has_prev = d > 0
    has_next = d < n_dom - 1

    loads = [
        pltpu.make_async_copy(src, dst, load_sem.at[i])
        for i, (src, dst) in enumerate(
            [
                (bnd_in, bnd),
                (feat_in, feat),
                (nbr_in, nbr),
                (anch_in, anch),
                (neg_in, neg),
                (pos_in, pos),
                (ws_in, ws),
                (wn_in, wn),
            ]
        )
    ]

    barrier = pltpu.get_barrier_semaphore()

    @pl.when(has_prev)
    def _():
        pl.semaphore_signal(barrier, inc=1, device_id=(d - 1, w), device_id_type=MESH)

    @pl.when(has_next)
    def _():
        pl.semaphore_signal(barrier, inc=1, device_id=(d + 1, w), device_id_type=MESH)

    partner = [peer_at(w, o, n_wide) for o in range(n_wide)]
    origin = partner if n_wide & (n_wide - 1) == 0 else [peer_at(w, -o, n_wide) for o in range(n_wide)]
    for o in range(1, n_wide):
        pl.semaphore_signal(barrier, inc=1, device_id=(d, partner[o]), device_id_type=MESH)

    for load in loads[:2]:
        load.start()

    loads[0].wait()
    b_row = jnp.concatenate([bnd[0, 0:1, :], bnd[0, 1:2, :]], axis=1)
    b_pick = marks(b_row, node_dev).T.astype(BF)
    loads[1].wait()
    for load in loads[2:]:
        load.start()
    features = feat[...]
    picked = dot(b_pick, features)
    halves = b_send.shape[0]
    half = width // halves
    for h in range(halves):
        b_send[h] = picked[:, h * half : (h + 1) * half].astype(BF).reshape(2, bnd_rows, half)

    arrivals = n_wide - 1 + has_prev.astype(jnp.int32) + has_next.astype(jnp.int32)
    pl.semaphore_wait(barrier, arrivals)

    def boundary_copies(side, step):
        return [
            pltpu.make_async_remote_copy(
                src_ref=b_send.at[h, side],
                dst_ref=b_recv.at[h, side],
                send_sem=bs_sem.at[h, side],
                recv_sem=br_sem.at[h, side],
                device_id=(d + step, w),
                device_id_type=MESH,
            )
            for h in range(halves)
        ]

    up = boundary_copies(0, 1)
    down = boundary_copies(1, -1)
    even = lax.rem(d, 2) == 0
    for h in range(halves):

        @pl.when(jnp.logical_and(has_prev, even))
        def _():
            down[h].start()

        @pl.when(has_next)
        def _():
            up[h].start()

        @pl.when(jnp.logical_and(has_prev, jnp.logical_not(even)))
        def _():
            down[h].start()

    for h in range(halves):

        @pl.when(jnp.logical_not(has_prev))
        def _():
            b_recv[h, 0] = jnp.zeros((bnd_rows, half), BF)

        @pl.when(jnp.logical_not(has_next))
        def _():
            b_recv[h, 1] = jnp.zeros((bnd_rows, half), BF)

    loads[2].wait()
    table_rows = node_dev + 2 * bnd_rows
    counts_t = marks(nbr[0:1, :], table_rows)
    for slot in range(1, slots):
        counts_t = counts_t + marks(nbr[slot : slot + 1, :], table_rows)
    counts = counts_t.T.astype(BF)

    loads[3].wait()
    a_row = jnp.concatenate([anch[v : v + 1, :] for v in range(peers)], axis=1)
    anchors_t = marks(a_row, node_dev)
    anchors_n = anchors_t.T.astype(BF)
    anchors_t = anchors_t.astype(BF)
    n_anch = peers * anch_n
    picked_counts = dot(anchors_n, counts)
    counts_a = picked_counts.astype(BF)
    inverse_a = 1.0 / jnp.sum(picked_counts, axis=1, keepdims=True)
    inverse = 1.0 / jnp.sum(counts.astype(F32), axis=1, keepdims=True)
    both = jnp.concatenate([counts_a[:, :node_dev], counts[:, :node_dev]], axis=0)
    own_sum[...] = dot(both, features)

    loads[6].wait()
    feat_a = dot(anchors_n, features).astype(BF)
    own_proj[...] = dot(jnp.concatenate([feat_a, features], axis=0), ws[...])

    loads[4].wait()
    n_rows = jnp.concatenate([neg[v] for v in range(peers)], axis=1)
    mult_t = marks(n_rows[0:1, :], node_dev)
    for k in range(1, fan):
        mult_t = mult_t + marks(n_rows[k : k + 1, :], node_dev)
    mult[...] = mult_t.T.reshape(peers, anch_n, node_dev)
    loads[5].wait()
    first = marks(pos[0:1, :], node_dev).astype(BF)
    second = marks(pos[1:2, :], node_dev).astype(BF)
    pairs = dot_nt(
        jnp.concatenate([first, second], axis=1), jnp.concatenate([second, first], axis=1)
    )
    loads[7].wait()

    counts_bnd = jnp.concatenate([counts_a[:, node_dev:], counts[:, node_dev:]], axis=0)
    inverse_both = jnp.concatenate([inverse_a, inverse], axis=0)

    def projected(rows, h):
        cols = slice(h * half, (h + 1) * half)
        received = b_recv[h].reshape(2 * bnd_rows, half)
        total = own_sum[rows, cols] + dot(counts_bnd[rows, :], received)
        mean = (total * inverse_both[rows, :]).astype(BF)
        return own_proj[rows, :] + dot(mean, wn[cols, :])

    for h in range(halves):

        @pl.when(has_prev)
        def _():
            up[h].wait_recv()

        @pl.when(has_next)
        def _():
            down[h].wait_recv()

        if h < halves - 1:
            own_proj[...] = projected(slice(0, n_anch + node_dev), h)

    anchor_embed = projected(slice(0, n_anch), halves - 1).astype(BF)
    a_send[...] = anchor_embed.reshape(peers, anch_n, width)

    def exchange(source, target, send, recv, to):
        return [
            pltpu.make_async_remote_copy(
                src_ref=source.at[to[o]],
                dst_ref=target.at[w],
                send_sem=send.at[o - 1],
                recv_sem=recv.at[o - 1],
                device_id=(d, to[o]),
                device_id_type=MESH,
            )
            for o in range(1, n_wide)
        ]

    out = exchange(a_send, a_recv, as_sem, ar_sem, partner)
    for copy in out:
        copy.start()
    a_recv[pl.ds(w, 1)] = a_send[pl.ds(w, 1)]

    embed = projected(slice(n_anch, n_anch + node_dev), halves - 1).astype(BF)
    embed_v[...] = embed
    embed_t[...] = embed.T

    back = exchange(t_send, t_recv, ts_sem, tr_sem, origin)

    def answer(v):
        score = dot(a_recv[v], embed_t[...]) * scale
        c = (mult[v] * jax.nn.sigmoid(score)).astype(BF)
        coef[v] = c
        return dot(c, embed).astype(BF)

    t_recv[w] = answer(w)
    for copy, reply, v in zip(out, back, origin[1:]):
        copy.wait_recv()
        t_send[v] = answer(v)
        reply.start()

    c_pos = pairs * (jax.nn.sigmoid(dot(embed, embed_t[...]) * scale) - 1.0)
    got = a_recv[...].reshape(n_anch, width)
    grad = dot(c_pos.astype(BF), embed) + dot_tn(coef[...].reshape(n_anch, node_dev), got)
    for copy in back:
        copy.wait_recv()
    terms = t_recv[...].reshape(n_anch, width)
    grad_v[...] = (grad + dot(anchors_t, terms)).astype(BF)

    for h in range(halves):

        @pl.when(has_next)
        def _():
            up[h].wait_send()

        @pl.when(has_prev)
        def _():
            down[h].wait_send()

    for copy in out + back:
        copy.wait_send()


def store_kernel(embed_v, grad_v, embed_out, grad_out, sem):
    stores = [
        pltpu.make_async_copy(embed_v, embed_out, sem.at[0]),
        pltpu.make_async_copy(grad_v, grad_out, sem.at[1]),
    ]
    for store in stores:
        store.start()
    for store in stores:
        store.wait()


def body(n_dom, n_wide, features, w_self, w_neigh, boundary, neighbors, anchors, negatives, positives):
    node_dev, width = features.shape
    bnd_rows = boundary.shape[2]
    peers, anch_n = anchors.shape
    small = [boundary, neighbors.T, anchors, negatives.transpose(0, 2, 1), positives.T]
    block = (peers, anch_n, width)
    far = pl.BlockSpec(memory_space=pltpu.HBM)
    near = pl.BlockSpec(memory_space=pltpu.VMEM)
    results = [jax.ShapeDtypeStruct((node_dev, width), BF)] * 2
    held = pl.pallas_call(
        functools.partial(kernel, n_dom, n_wide),
        out_shape=[pltpu.VMEM((node_dev, width), BF)] * 2,
        in_specs=[far] * 8,
        out_specs=[near] * 2,
        scratch_shapes=[
            pltpu.VMEM(features.shape, BF),
            pltpu.VMEM(w_self.shape, BF),
            pltpu.VMEM(w_neigh.shape, BF),
        ]
        + [pltpu.VMEM(x.shape, jnp.int32) for x in small]
        + [pltpu.VMEM((2, 2, bnd_rows, width // 2), BF)] * 2
        + [pltpu.VMEM(block, BF)] * 4
        + [
            pltpu.VMEM((peers, anch_n, node_dev), F32),
            pltpu.VMEM((peers, anch_n, node_dev), BF),
            pltpu.VMEM((width, node_dev), BF),
        ]
        + [pltpu.VMEM((peers * anch_n + node_dev, width), F32)] * 2
        + [
            pltpu.SemaphoreType.DMA((8,)),
            pltpu.SemaphoreType.DMA((2, 2)),
            pltpu.SemaphoreType.DMA((2, 2)),
        ]
        + [pltpu.SemaphoreType.DMA((n_wide - 1,))] * 4,
        compiler_params=pltpu.CompilerParams(
            collective_id=0, has_side_effects=True, vmem_limit_bytes=32 * 1024 * 1024
        ),
    )(*[pltpu.with_memory_space_constraint(x, pltpu.HBM) for x in (features, w_self, w_neigh, *small)])
    return pl.pallas_call(
        store_kernel,
        out_shape=results,
        in_specs=[near] * 2,
        out_specs=[far] * 2,
        scratch_shapes=[pltpu.SemaphoreType.DMA((2,))],
        compiler_params=pltpu.CompilerParams(vmem_limit_bytes=4 * 1024 * 1024),
    )(*[pltpu.with_memory_space_constraint(x, pltpu.VMEM) for x in held])


def solution(mesh):
    return jax.shard_map(
        functools.partial(body, mesh.shape["dom"], mesh.shape["wide"]),
        mesh=mesh,
        in_specs=(
            P(("dom", "wide"), None),
            P(),
            P(),
            P(("dom", "wide"), None, None),
            P(("dom", "wide"), None),
            P(("dom", "wide"), None),
            P(("dom", "wide"), None, None),
            P(("dom", "wide"), None),
        ),
        out_specs=(P(("dom", "wide"), None), P(("dom", "wide"), None)),
        check_vma=False,
    )
```

```python
import functools
import math

import jax
import jax.numpy as jnp
from jax import lax
from jax.experimental import pallas as pl
from jax.experimental.pallas import tpu as pltpu
from jax.sharding import PartitionSpec as P

MESH = pl.DeviceIdType.MESH
BF = jnp.bfloat16
F32 = jnp.float32


def dot(a, b):
    return jnp.dot(a, b, preferred_element_type=F32)


def dot_nt(a, b):
    return lax.dot_general(a, b, (((1,), (1,)), ((), ())), preferred_element_type=F32)


def dot_tn(a, b):
    return lax.dot_general(a, b, (((0,), (0,)), ((), ())), preferred_element_type=F32)


def marks(row, height):
    rows = lax.broadcasted_iota(jnp.int32, (height, row.shape[1]), 0)
    return jnp.where(rows == row, 1.0, 0.0)


def peer_at(w, o, n):
    if n & (n - 1):
        return lax.rem(w + o + n, n)
    bit = 1
    while bit <= o:
        if o & bit:
            w = w + bit * (1 - 2 * lax.rem(w // bit, 2))
        bit *= 2
    return w


def kernel(
    n_dom,
    n_wide,
    feat_in,
    ws_in,
    wn_in,
    bnd_in,
    nbr_in,
    anch_in,
    neg_in,
    pos_in,
    embed_v,
    grad_v,
    feat,
    ws,
    wn,
    bnd,
    nbr,
    anch,
    neg,
    pos,
    b_send,
    b_recv,
    a_send,
    a_recv,
    t_send,
    t_recv,
    mult,
    coef,
    embed_t,
    own_sum,
    own_proj,
    load_sem,
    bs_sem,
    br_sem,
    as_sem,
    ar_sem,
    ts_sem,
    tr_sem,
):
    node_dev, width = feat.shape
    slots = nbr.shape[0]
    bnd_rows = bnd.shape[2]
    peers, anch_n = anch.shape
    fan = neg.shape[1]
    scale = 1.0 / math.sqrt(width)
    d = lax.axis_index("dom")
    w = lax.axis_index("wide")
    has_prev = d > 0
    has_next = d < n_dom - 1

    loads = [
        pltpu.make_async_copy(src, dst, load_sem.at[i])
        for i, (src, dst) in enumerate(
            [
                (bnd_in, bnd),
                (feat_in, feat),
                (nbr_in, nbr),
                (anch_in, anch),
                (neg_in, neg),
                (pos_in, pos),
                (ws_in, ws),
                (wn_in, wn),
            ]
        )
    ]
    for load in loads[:2]:
        load.start()

    barrier = pltpu.get_barrier_semaphore()

    @pl.when(has_prev)
    def _():
        pl.semaphore_signal(barrier, inc=1, device_id=(d - 1, w), device_id_type=MESH)

    @pl.when(has_next)
    def _():
        pl.semaphore_signal(barrier, inc=1, device_id=(d + 1, w), device_id_type=MESH)

    partner = [peer_at(w, o, n_wide) for o in range(n_wide)]
    origin = partner if n_wide & (n_wide - 1) == 0 else [peer_at(w, -o, n_wide) for o in range(n_wide)]
    for o in range(1, n_wide):
        pl.semaphore_signal(barrier, inc=1, device_id=(d, partner[o]), device_id_type=MESH)

    loads[0].wait()
    b_row = jnp.concatenate([bnd[0, 0:1, :], bnd[0, 1:2, :]], axis=1)
    b_pick = marks(b_row, node_dev).T.astype(BF)
    loads[1].wait()
    for load in loads[2:]:
        load.start()
    features = feat[...]
    picked = dot(b_pick, features)
    b_send[...] = picked.astype(BF).reshape(2, bnd_rows, width)

    arrivals = n_wide - 1 + has_prev.astype(jnp.int32) + has_next.astype(jnp.int32)
    pl.semaphore_wait(barrier, arrivals)

    up = pltpu.make_async_remote_copy(
        src_ref=b_send.at[0],
        dst_ref=b_recv.at[0],
        send_sem=bs_sem.at[0],
        recv_sem=br_sem.at[0],
        device_id=(d + 1, w),
        device_id_type=MESH,
    )
    down = pltpu.make_async_remote_copy(
        src_ref=b_send.at[1],
        dst_ref=b_recv.at[1],
        send_sem=bs_sem.at[1],
        recv_sem=br_sem.at[1],
        device_id=(d - 1, w),
        device_id_type=MESH,
    )

    even = lax.rem(d, 2) == 0

    @pl.when(jnp.logical_and(has_prev, even))
    def _():
        down.start()

    @pl.when(has_next)
    def _():
        up.start()

    @pl.when(jnp.logical_and(has_prev, jnp.logical_not(even)))
    def _():
        down.start()

    @pl.when(jnp.logical_not(has_prev))
    def _():
        b_recv[0] = jnp.zeros((bnd_rows, width), BF)

    @pl.when(jnp.logical_not(has_next))
    def _():
        b_recv[1] = jnp.zeros((bnd_rows, width), BF)

    loads[2].wait()
    table_rows = node_dev + 2 * bnd_rows
    counts_t = marks(nbr[0:1, :], table_rows)
    for slot in range(1, slots):
        counts_t = counts_t + marks(nbr[slot : slot + 1, :], table_rows)
    counts = counts_t.T.astype(BF)

    loads[3].wait()
    a_row = jnp.concatenate([anch[v : v + 1, :] for v in range(peers)], axis=1)
    anchors_t = marks(a_row, node_dev)
    anchors_n = anchors_t.T.astype(BF)
    anchors_t = anchors_t.astype(BF)
    n_anch = peers * anch_n
    picked_counts = dot(anchors_n, counts)
    counts_a = picked_counts.astype(BF)
    inverse_a = 1.0 / jnp.sum(picked_counts, axis=1, keepdims=True)
    inverse = 1.0 / jnp.sum(counts.astype(F32), axis=1, keepdims=True)
    both = jnp.concatenate([counts_a[:, :node_dev], counts[:, :node_dev]], axis=0)
    own_sum[...] = dot(both, features)

    loads[6].wait()
    feat_a = dot(anchors_n, features).astype(BF)
    own_proj[...] = dot(jnp.concatenate([feat_a, features], axis=0), ws[...])

    loads[4].wait()
    n_rows = jnp.concatenate([neg[v] for v in range(peers)], axis=1)
    mult_t = marks(n_rows[0:1, :], node_dev)
    for k in range(1, fan):
        mult_t = mult_t + marks(n_rows[k : k + 1, :], node_dev)
    mult[...] = mult_t.T.reshape(peers, anch_n, node_dev)
    loads[7].wait()

    @pl.when(has_prev)
    def _():
        up.wait_recv()

    @pl.when(has_next)
    def _():
        down.wait_recv()

    received = b_recv[...].reshape(2 * bnd_rows, width)

    def embedding(rows, bnd_counts, inv):
        mean = ((own_sum[rows, :] + dot(bnd_counts, received)) * inv).astype(BF)
        return (own_proj[rows, :] + dot(mean, wn[...])).astype(BF)

    anchor_embed = embedding(pl.ds(0, n_anch), counts_a[:, node_dev:], inverse_a)
    a_send[...] = anchor_embed.reshape(peers, anch_n, width)

    def exchange(source, target, send, recv, to):
        return [
            pltpu.make_async_remote_copy(
                src_ref=source.at[to[o]],
                dst_ref=target.at[w],
                send_sem=send.at[o - 1],
                recv_sem=recv.at[o - 1],
                device_id=(d, to[o]),
                device_id_type=MESH,
            )
            for o in range(1, n_wide)
        ]

    out = exchange(a_send, a_recv, as_sem, ar_sem, partner)
    for copy in out:
        copy.start()
    a_recv[pl.ds(w, 1)] = a_send[pl.ds(w, 1)]

    embed = embedding(pl.ds(n_anch, node_dev), counts[:, node_dev:], inverse)
    embed_v[...] = embed
    embed_t[...] = embed.T

    back = exchange(t_send, t_recv, ts_sem, tr_sem, origin)

    def answer(v):
        score = dot(a_recv[v], embed_t[...]) * scale
        c = (mult[v] * jax.nn.sigmoid(score)).astype(BF)
        coef[v] = c
        return dot(c, embed).astype(BF)

    for copy, reply, v in list(zip(out, back, origin[1:]))[:1]:
        copy.wait_recv()
        t_send[v] = answer(v)
        reply.start()

    far = list(zip(out, back, origin[1:]))[1:]
    for copy, _, v in far:
        copy.wait_recv()
    if far:
        blocks = jnp.concatenate([a_recv[v] for _, _, v in far], axis=0)
        counted = jnp.concatenate([mult[v] for _, _, v in far], axis=0)
        c_far = (counted * jax.nn.sigmoid(dot(blocks, embed_t[...]) * scale)).astype(BF)
        t_far = dot(c_far, embed).astype(BF)
    for i, (_, reply, v) in enumerate(far):
        t_send[v] = t_far[i * anch_n : (i + 1) * anch_n]
        coef[v] = c_far[i * anch_n : (i + 1) * anch_n]
        reply.start()

    loads[5].wait()
    first = marks(pos[0:1, :], node_dev).astype(BF)
    second = marks(pos[1:2, :], node_dev).astype(BF)
    pairs = dot_nt(
        jnp.concatenate([first, second], axis=1), jnp.concatenate([second, first], axis=1)
    )
    t_recv[w] = answer(w)
    c_pos = pairs * (jax.nn.sigmoid(dot(embed, embed_t[...]) * scale) - 1.0)
    got = a_recv[...].reshape(n_anch, width)
    grad = dot(c_pos.astype(BF), embed) + dot_tn(coef[...].reshape(n_anch, node_dev), got)
    for copy in back:
        copy.wait_recv()
    terms = t_recv[...].reshape(n_anch, width)
    grad_v[...] = (grad + dot(anchors_t, terms)).astype(BF)

    @pl.when(has_next)
    def _():
        up.wait_send()

    @pl.when(has_prev)
    def _():
        down.wait_send()

    for copy in out + back:
        copy.wait_send()


def store_kernel(embed_v, grad_v, embed_out, grad_out, sem):
    stores = [
        pltpu.make_async_copy(embed_v, embed_out, sem.at[0]),
        pltpu.make_async_copy(grad_v, grad_out, sem.at[1]),
    ]
    for store in stores:
        store.start()
    for store in stores:
        store.wait()


def body(n_dom, n_wide, features, w_self, w_neigh, boundary, neighbors, anchors, negatives, positives):
    node_dev, width = features.shape
    bnd_rows = boundary.shape[2]
    peers, anch_n = anchors.shape
    small = [boundary, neighbors.T, anchors, negatives.transpose(0, 2, 1), positives.T]
    block = (peers, anch_n, width)
    far = pl.BlockSpec(memory_space=pltpu.HBM)
    near = pl.BlockSpec(memory_space=pltpu.VMEM)
    results = [jax.ShapeDtypeStruct((node_dev, width), BF)] * 2
    held = pl.pallas_call(
        functools.partial(kernel, n_dom, n_wide),
        out_shape=[pltpu.VMEM((node_dev, width), BF)] * 2,
        in_specs=[far] * 8,
        out_specs=[near] * 2,
        scratch_shapes=[
            pltpu.VMEM(features.shape, BF),
            pltpu.VMEM(w_self.shape, BF),
            pltpu.VMEM(w_neigh.shape, BF),
        ]
        + [pltpu.VMEM(x.shape, jnp.int32) for x in small]
        + [pltpu.VMEM((2, bnd_rows, width), BF)] * 2
        + [pltpu.VMEM(block, BF)] * 4
        + [
            pltpu.VMEM((peers, anch_n, node_dev), F32),
            pltpu.VMEM((peers, anch_n, node_dev), BF),
            pltpu.VMEM((width, node_dev), BF),
        ]
        + [pltpu.VMEM((peers * anch_n + node_dev, width), F32)] * 2
        + [
            pltpu.SemaphoreType.DMA((8,)),
            pltpu.SemaphoreType.DMA((2,)),
            pltpu.SemaphoreType.DMA((2,)),
        ]
        + [pltpu.SemaphoreType.DMA((n_wide - 1,))] * 4,
        compiler_params=pltpu.CompilerParams(
            collective_id=0, has_side_effects=True, vmem_limit_bytes=32 * 1024 * 1024
        ),
    )(*[pltpu.with_memory_space_constraint(x, pltpu.HBM) for x in (features, w_self, w_neigh, *small)])
    return pl.pallas_call(
        store_kernel,
        out_shape=results,
        in_specs=[near] * 2,
        out_specs=[far] * 2,
        scratch_shapes=[pltpu.SemaphoreType.DMA((2,))],
        compiler_params=pltpu.CompilerParams(vmem_limit_bytes=4 * 1024 * 1024),
    )(*[pltpu.with_memory_space_constraint(x, pltpu.VMEM) for x in held])


def solution(mesh):
    return jax.shard_map(
        functools.partial(body, mesh.shape["dom"], mesh.shape["wide"]),
        mesh=mesh,
        in_specs=(
            P(("dom", "wide"), None),
            P(),
            P(),
            P(("dom", "wide"), None, None),
            P(("dom", "wide"), None),
            P(("dom", "wide"), None),
            P(("dom", "wide"), None, None),
            P(("dom", "wide"), None),
        ),
        out_specs=(P(("dom", "wide"), None), P(("dom", "wide"), None)),
        check_vma=False,
    )
```
